256 devices in a mesh: dp: 16 (over z, core), tensor: 16 (over y, x).
Axes of the slice: x: 4, y: 4, z: 8, core: 2. Of those that a mesh axis runs over, the one named last changes fastest.
Arguments:
- tokens: bfloat16 [8192, 8192], P('dp', 'tensor'), may hold values from -6 to 6
- weight: bfloat16 [8192, 8192], P('tensor'), may hold values from -0.0625 to 0.0625
- down_adapter: bfloat16 [8192, 16], P('tensor'), may hold values from -0.0625 to 0.0625
- up_adapter: bfloat16 [16, 8192], replicated, may hold values from -0.29882812 to 0.29882812
- cotangent: bfloat16 [8192, 8192], P(('dp', 'tensor')), may hold values from -6 to 6
Outputs:
- output: bfloat16 [8192, 8192], P(('dp', 'tensor'))
- token_gradient: bfloat16 [8192, 8192], P('dp', 'tensor')
- grad_a: float32 [8192, 16], P('tensor')
- grad_b: float32 [16, 8192], replicated
The draws below stay inside these ranges and needn't reach their ends.
All inputs are finite; a program needn't handle non-finite values.
Results may differ from the reference program's by a relative error of at most 0.0029.
Values may be sent and summed in bfloat16 or wider, within the bound.
A program may use at most 128 MiB of HBM per device.

```python
import math
import jax
import jax.numpy as jnp

D = 8192
R = 16
TOKEN_TOTAL = 8192


def levels(own_key, extent, split, smallest, high):
    level, own = 1.0, jax.random.fold_in(own_key, 6)
    for position, parts in split:
        steps = jnp.exp(jax.random.uniform(jax.random.fold_in(own, position), (parts,), jnp.float32, smallest / len(split), high / len(split)))
        level = level * jnp.repeat(steps, extent[position] // parts).reshape([-1 if axis == position else 1 for axis in range(len(extent))])
    return level


def scatter_about(rng, dims, width, reach, pieces=(), held_as=jnp.bfloat16):
    level = levels(rng, dims, pieces, -0.22, 0.18) if pieces else 1.0
    result = jax.random.normal(rng, dims, jnp.float32) * width * level
    return jnp.minimum(jnp.maximum(result, -reach), reach).astype(held_as)


def setup_inputs(seed: int = 0) -> dict:
    arg_keys = jax.random.split(jax.random.key(seed), 6)
    return {
        "tokens": scatter_about(arg_keys[0], (TOKEN_TOTAL, D), 1.0, 6.0, ((0, 16), (1, 16))),
        "weight": scatter_about(arg_keys[1], (D, D), D ** -0.5, 0.0625, ((0, 16),)),
        "down_adapter": scatter_about(arg_keys[2], (D, R), D ** -0.5, 0.0625, ((0, 16),)),
        "up_adapter": scatter_about(arg_keys[3], (R, D), 0.05, 0.29882812),
        "cotangent": scatter_about(arg_keys[4], (TOKEN_TOTAL, D), 1.0, 6.0, ((0, 256),)),
    }


adapter_scale = 0.5

def reference(tokens, weight, down_adapter, up_adapter, cotangent):
    frozen_output = jnp.dot(tokens, weight, preferred_element_type=jnp.float32)
    narrow_output = jnp.dot(tokens, down_adapter, preferred_element_type=jnp.float32).astype(jnp.bfloat16)
    output = (frozen_output + adapter_scale * jnp.dot(narrow_output, up_adapter, preferred_element_type=jnp.float32)).astype(jnp.bfloat16)
    narrow_gradient = jnp.dot(cotangent, up_adapter.T, preferred_element_type=jnp.float32).astype(jnp.bfloat16)
    token_gradient = (jnp.dot(cotangent, weight.T, preferred_element_type=jnp.float32) + adapter_scale * jnp.dot(narrow_gradient, down_adapter.T, preferred_element_type=jnp.float32)).astype(jnp.bfloat16)
    gradient_factor = adapter_scale / math.sqrt(TOKEN_TOTAL)
    grad_a = gradient_factor * jnp.dot(tokens.T, narrow_gradient, preferred_element_type=jnp.float32)
    grad_b = gradient_factor * jnp.dot(narrow_output.T, cotangent, preferred_element_type=jnp.float32)
    return (output, token_gradient, grad_a, grad_b)
```

```python
import functools
import math

import jax
import jax.numpy as jnp
from jax import lax
from jax.experimental import pallas as pl
from jax.experimental.pallas import tpu as pltpu
from jax.sharding import PartitionSpec as P

MESH = pl.DeviceIdType.MESH
F32, BF16 = jnp.float32, jnp.bfloat16
SCALE = 0.5
FACTOR = SCALE / math.sqrt(8192)
CHUNKS, CW = 4, 512
HOPS = ((4, 3), (3, 4))


def dot(a, b, da, db):
    return lax.dot_general(a, b, (((da,), (db,)), ((), ())), preferred_element_type=F32)


def kernel(tok, w, down, up, cot, out, tg, ga, gb,
           wg, tokg, cotg, upv, dnv, lx, ly, lowv, lgx, lgv, of, os, orx, ob, gf, gs, gr, tgv, gab, sibin, zin, gav,
           loc, wa_s, wa_r, wz_s, wz_r, ws_s, ws_r, c1_s, c1_r, c2_s, c2_r, t_s, t_r, lx_s, lx_r, ly_s, ly_r,
           lgx_s, lgx_r, lgy_s, lgy_r, o1_s, o1_r, o2_s, o2_r, g_s, g_r, sb_s, sb_r, z_s, z_r, gy_s, gy_r, gx_s, gx_r):
    dp, t = lax.axis_index("dp"), lax.axis_index("tensor")
    z, c = lax.div(dp, 2), lax.rem(dp, 2)
    y, x = lax.div(t, 4), lax.rem(t, 4)

    def row(d):
        return (dp, y * 4 + lax.rem(x + d, 4))

    def col(d):
        return (dp, lax.rem(y + d, 4) * 4 + x)

    def zed(d):
        return (lax.rem(z + d, 8) * 2 + c, t)

    sib = (z * 2 + 1 - c, t)
    sends = []

    def rc(src, dst, ss, rs, dev):
        return pltpu.make_async_remote_copy(src, dst, ss, rs, device_id=dev, device_id_type=MESH)

    def push(*a):
        cp = rc(*a)
        cp.start()
        sends.append(cp)
        return cp

    def local(src, dst, i):
        cp = pltpu.make_async_copy(src, dst, loc.at[i])
        cp.start()
        return cp

    def slab(i, size):
        return pl.ds(pl.multiple_of(i * size, size), size)

    ld_tok = local(tok, tokg.at[:, pl.ds(0, 512)], 0)
    ld_dn = local(down, dnv, 1)
    ld_up = local(up.at[:, slab(x, 2048)], upv, 2)
    ld_cot = local(cot.at[:, slab(x, 2048)], cotg.at[0, slab(x, 32), :], 3)
    ld_w = local(w.at[:, slab(x, 2048)], wg.at[0], 4)

    bar = pltpu.get_barrier_semaphore()
    peers = [row(d) for d in (1, 2, 3)] + [col(d) for d in (1, 2, 3)] + [zed(d) for d in range(1, 8)] + [sib]
    for dev in peers:
        pl.semaphore_signal(bar, inc=1, device_id=dev, device_id_type=MESH)
    pl.semaphore_wait(bar, len(peers))

    wa = [[None] * 4 for _ in range(CHUNKS)]
    c1 = [None] * 4

    def send_w(j):
        for d in (2, 1, 3):
            n0 = pl.multiple_of(lax.rem(x + d, 4) * 2048 + j * CW, CW)
            wa[j][d] = push(w.at[slab(dp, 32), pl.ds(n0, CW)],
                            wg.at[4 - d, slab(dp, 32), pl.ds(j * CW, CW)], wa_s.at[j, d], wa_r.at[j, d], row(d))

    send_w(0)
    for d in (2, 1, 3):
        c1[d] = push(cot.at[:, slab(lax.rem(x + d, 4), 2048)], cotg.at[0, slab(x, 32), :], c1_s.at[d], c1_r.at[d], row(d))
    for j in range(1, CHUNKS):
        send_w(j)

    ld_tok.wait()
    ld_dn.wait()
    lx[0] = dot(dnv[...], tokg[:, pl.ds(0, 512)], 1, 1)
    lxc = [None] + [push(lx.at[0], lx.at[4 - d], lx_s.at[d], lx_r.at[d], row(d)) for d in (1, 2, 3)]

    ld_cot.wait()
    for d in (1, 2, 3):
        rc(cotg.at[0, slab(x, 32), :], cotg.at[0, slab(lax.rem(x + 4 - d, 4), 32), :], c1_s.at[d], c1_r.at[d],
           row(d)).wait_recv()
    c2 = [None] + [push(cotg.at[0], cotg.at[4 - d], c2_s.at[d], c2_r.at[d], col(d)) for d in (1, 2, 3)]
    tc = [None] + [push(tok, tokg.at[:, pl.ds((4 - d) * 512, 512)], t_s.at[d], t_r.at[d], row(d)) for d in (1, 2, 3)]
    ld_up.wait()
    lgx[0] = dot(upv[...], cotg[0], 1, 1)
    lgxc = [None] + [push(lgx.at[0], lgx.at[4 - d], lgx_s.at[d], lgx_r.at[d], row(d)) for d in (1, 2, 3)]

    def part(zz, cc, j):
        return wg.at[pl.ds(1, 3), slab(zz * 2 + cc, 32), pl.ds(j * CW, CW)]

    def origin(up_, s):
        return lax.rem(z + (8 - s if up_ else s), 8)

    def to_sib(zz, j, i):
        push(part(zz, c, j), part(zz, c, j), ws_s.at[j, i], ws_r.at[j, i], sib)

    def send_z(zz, j, k, s):
        push(part(zz, c, j), part(zz, c, j), wz_s.at[k, j, s], wz_r.at[k, j, s], zed(1 if k == 0 else 7))

    def small_low():
        for d in (1, 2, 3):
            lxc[d].wait_recv()
        ly[0] = (lx[0] + lx[1]) + (lx[2] + lx[3])
        return [None] + [push(ly.at[0], ly.at[4 - d], ly_s.at[d], ly_r.at[d], col(d)) for d in (1, 2, 3)]

    def small_lg():
        for d in (1, 2, 3):
            lgxc[d].wait_recv()
        lgv[0] = ((lgx[0] + lgx[1]) + (lgx[2] + lgx[3])).astype(BF16)
        return [None] + [push(lgv.at[0], lgv.at[4 - d], lgy_s.at[d], lgy_r.at[d], col(d)) for d in (1, 2, 3)]

    for pair in ((0, 1), (2, 3)):
        for j in pair:
            for d in (1, 2, 3):
                wa[j][d].wait_recv()
            send_z(z, j, 0, 1)
            send_z(z, j, 1, 1)
            to_sib(z, j, 0)
        if pair[0] == 0:
            lyc = small_low()
            lgyc = small_lg()
        for s in range(1, 5):
            for j in pair:
                for k in (0, 1):
                    if s > HOPS[j % 2][k]:
                        continue
                    zz = origin(k == 0, s)
                    rc(part(zz, c, j), part(zz, c, j), wz_s.at[k, j, s], wz_r.at[k, j, s], zed(1)).wait_recv()
                    if s < HOPS[j % 2][k]:
                        send_z(zz, j, k, s + 1)
                    to_sib(zz, j, s if k == 0 else 4 + s)

    def wait_sib(j):
        rc(part(z, c, j), part(z, 1 - c, j), ws_s.at[j, 0], ws_r.at[j, 0], sib).wait_recv()
        for k in (0, 1):
            for s in range(1, HOPS[j % 2][k] + 1):
                zz, i = origin(k == 0, s), (s if k == 0 else 4 + s)
                rc(part(zz, c, j), part(zz, 1 - c, j), ws_s.at[j, i], ws_r.at[j, i], sib).wait_recv()

    for d in (1, 2, 3):
        lyc[d].wait_recv()
        lgyc[d].wait_recv()
    lowv[...] = ((ly[0] + ly[1]) + (ly[2] + ly[3])).astype(BF16)

    ld_w.wait()
    for d in (1, 2, 3):
        tc[d].wait_recv()
    o1 = [[None] * 4 for _ in range(CHUNKS)]
    for j in range(CHUNKS):
        wait_sib(j)

        @pl.loop(0, 2)
        def _(q):
            cols = slab(j * 2 + q, 256)
            acc = dot(tokg[...], wg[:, :, cols].reshape(2048, 256), 1, 0)
            of[:, cols] = acc
            os[:, cols] = acc.astype(BF16)

        for d in (2, 1, 3):
            o1[j][d] = push(os.at[slab(lax.rem(y + d, 4), 128), pl.ds(j * CW, CW)], orx.at[3 - d, :, pl.ds(j * CW, CW)],
                            o1_s.at[j, d], o1_r.at[j, d], col(d))

    for d in (1, 2, 3):
        c2[d].wait_recv()
    gc = [[None] * 2 for _ in range(4)]
    for r in (2, 1, 3):
        for h in range(2):
            acc = dot(cotg[...].reshape(512, 2048), wg[r, pl.ds(h * 256, 256), :], 1, 1)
            gs[r - 1, :, pl.ds(h * 256, 256)] = acc.astype(BF16)
            gc[r][h] = push(gs.at[r - 1, :, pl.ds(h * 256, 256)], gr.at[3 - r, :, pl.ds(h * 256, 256)],
                            g_s.at[r, h], g_r.at[r, h], row(r))

    parts_a = [dot(lgv[r], tokg[slab(lax.rem(y + r, 4), 128), pl.ds(0, 512)], 1, 0) for r in range(4)]
    gab[0] = (parts_a[0] + parts_a[1]) + (parts_a[2] + parts_a[3])
    parts_b = [dot(lowv[:, slab(lax.rem(y + r, 4), 128)], cotg[r, :, slab(y, 512)], 1, 0) for r in range(4)]
    gab[1] = (parts_b[0] + parts_b[1]) + (parts_b[2] + parts_b[3])
    sb0 = push(gab.at[1 - c], sibin, sb_s.at[0], sb_r.at[0], sib)

    for h in range(2):
        gf[:, pl.ds(h * 256, 256)] = dot(cotg[...].reshape(512, 2048), wg[0, pl.ds(h * 256, 256), :], 1, 1)

    sb0.wait_recv()
    zin[z] = gab[c] + sibin[...]
    zc = [None] + [push(zin.at[z], zin.at[z], z_s.at[d], z_r.at[d], zed(d)) for d in range(1, 8)]

    o2 = [[None] * 4 for _ in range(CHUNKS)]
    own = []
    for j in range(CHUNKS):
        cols = pl.ds(j * CW, CW)
        for d in (1, 2, 3):
            o1[j][d].wait_recv()
        acc = of[slab(y, 128), cols] + orx[0, :, cols].astype(F32) + orx[1, :, cols].astype(F32) + orx[2, :, cols].astype(F32)
        acc += SCALE * dot(lowv[:, slab(y, 128)], upv[:, cols], 0, 0)
        ob[:, cols] = acc.astype(BF16)
        here = pl.ds(pl.multiple_of(x * 2048 + j * CW, CW), CW)
        for d in (2, 1, 3):
            o2[j][d] = push(ob.at[slab(lax.rem(x + d, 4), 32), cols], out.at[:, here], o2_s.at[j, d], o2_r.at[j, d], row(d))
        own.append(local(ob.at[slab(x, 32), cols], out.at[:, here], 5 + j))

    for d in range(1, 8):
        rc(zin.at[z], zin.at[lax.rem(z + 8 - d, 8)], z_s.at[d], z_r.at[d], zed(d)).wait_recv()
    total = zin[0]
    for i in range(1, 8):
        total = total + zin[i]
    gab_t = gav
    gab_t[c] = total * FACTOR
    sb1 = push(gab_t.at[c], gab_t.at[c], sb_s.at[1], sb_r.at[1], sib)
    rc(gab_t.at[c], gab_t.at[1 - c], sb_s.at[1], sb_r.at[1], sib).wait_recv()
    half = slab(c, 8)
    mine = pl.ds(pl.multiple_of(x * 2048 + y * 512, 512), 512)
    gyc = [push(gab_t.at[1, half, :], gb.at[half, mine], gy_s.at[d], gy_r.at[d], col(d)) for d in (1, 2, 3)]
    gb_own = local(gab_t.at[1, half, :], gb.at[half, mine], 9)

    for h in range(2):
        cols = pl.ds(h * 256, 256)
        for r in (1, 2, 3):
            gc[r][h].wait_recv()
        for q in range(4):
            rows = pl.ds(q * 128, 128)
            acc = gf[rows, cols] + gr[0, rows, cols].astype(F32) + gr[1, rows, cols].astype(F32) + gr[2, rows, cols].astype(F32)
            acc += SCALE * dot(lgv[q], dnv[:, cols], 0, 0)
            tgv[slab(lax.rem(y + q, 4), 128), cols] = acc.astype(BF16)
    tg_out = local(tgv, tg, 10)

    gb_own.wait()
    for d, cp in zip((1, 2, 3), gyc):
        there = pl.ds(pl.multiple_of(x * 2048 + lax.rem(y + 4 - d, 4) * 512, 512), 512)
        rc(gab_t.at[1, half, :], gb.at[half, there], gy_s.at[d], gy_r.at[d], col(d)).wait_recv()
    quarter = slab(x, 2048)
    for d in (1, 2, 3):
        push(gb.at[half, quarter], gb.at[half, quarter], gx_s.at[d], gx_r.at[d], row(d))
    for d in (1, 2, 3):
        there = slab(lax.rem(x + 4 - d, 4), 2048)
        rc(gb.at[half, quarter], gb.at[half, there], gx_s.at[d], gx_r.at[d], row(d)).wait_recv()
    push(gb.at[half, :], gb.at[half, :], sb_s.at[2], sb_r.at[2], sib)
    ga_out = local(gab_t.at[0], ga, 11)
    rc(gb.at[half, :], gb.at[slab(1 - c, 8), :], sb_s.at[2], sb_r.at[2], sib).wait_recv()

    for j in range(CHUNKS):
        own[j].wait()
        for d in (1, 2, 3):
            there = pl.ds(pl.multiple_of(lax.rem(x + 4 - d, 4) * 2048 + j * CW, CW), CW)
            rc(ob.at[slab(0, 32), pl.ds(j * CW, CW)], out.at[:, there], o2_s.at[j, d], o2_r.at[j, d], row(d)).wait_recv()
    tg_out.wait()
    ga_out.wait()
    for cp in sends:
        cp.wait_send()


def per_device(tokens, weight, down_adapter, up_adapter, cotangent):
    dma = pltpu.SemaphoreType.DMA
    any_ = pl.BlockSpec(memory_space=pl.ANY)
    sems = [(12,)] + [(CHUNKS, 4)] * 2 + [(2, CHUNKS, 5)] * 2 + [(CHUNKS, 9)] * 2 + [(4,)] * 14
    sems += [(CHUNKS, 4)] * 4 + [(4, 2)] * 2 + [(3,)] * 2 + [(8,)] * 2 + [(4,)] * 4
    out, token_gradient, grad_a, grad_b = pl.pallas_call(
        kernel,
        out_shape=(
            jax.ShapeDtypeStruct((32, 8192), BF16),
            jax.ShapeDtypeStruct((512, 512), BF16),
            jax.ShapeDtypeStruct((16, 512), F32),
            jax.ShapeDtypeStruct((16, 8192), F32),
        ),
        in_specs=[any_] * 5,
        out_specs=(any_,) * 4,
        scratch_shapes=[
            pltpu.VMEM((4, 512, 2048), BF16),
            pltpu.VMEM((512, 2048), BF16),
            pltpu.VMEM((4, 128, 2048), BF16),
            pltpu.VMEM((16, 2048), BF16),
            pltpu.VMEM((16, 512), BF16),
            pltpu.VMEM((4, 16, 512), F32),
            pltpu.VMEM((4, 16, 512), F32),
            pltpu.VMEM((16, 512), BF16),
            pltpu.VMEM((4, 16, 128), F32),
            pltpu.VMEM((4, 16, 128), BF16),
            pltpu.VMEM((512, 2048), F32),
            pltpu.VMEM((512, 2048), BF16),
            pltpu.VMEM((3, 128, 2048), BF16),
            pltpu.VMEM((128, 2048), BF16),
            pltpu.VMEM((512, 512), F32),
            pltpu.VMEM((3, 512, 512), BF16),
            pltpu.VMEM((3, 512, 512), BF16),
            pltpu.VMEM((512, 512), BF16),
            pltpu.VMEM((2, 16, 512), F32),
            pltpu.VMEM((16, 512), F32),
            pltpu.VMEM((8, 16, 512), F32),
            pltpu.VMEM((2, 16, 512), F32),
        ] + [dma(s) for s in sems],
        compiler_params=pltpu.CompilerParams(
            collective_id=0, has_side_effects=True, vmem_limit_bytes=56 * 2**20
        ),
        name="projection",
    )(tokens, weight, down_adapter.T, up_adapter, cotangent)
    return out, token_gradient, grad_a.T, grad_b


def solution(mesh):
    placed = (
        P("dp", "tensor"),
        P("tensor", None),
        P("tensor", None),
        P(),
        P(("dp", "tensor"), None),
    )
    return jax.shard_map(
        per_device,
        mesh=mesh,
        in_specs=placed,
        out_specs=(P(("dp", "tensor"), None), P("dp", "tensor"), P("tensor", None), P()),
        check_vma=False,
    )
```

```python
import math

import jax
import jax.numpy as jnp
from jax import lax
from jax.experimental import pallas as pl
from jax.experimental.pallas import tpu as pltpu
from jax.sharding import PartitionSpec as P

MESH = pl.DeviceIdType.MESH
F32, BF16 = jnp.float32, jnp.bfloat16
SCALE = 0.5
FACTOR = SCALE / math.sqrt(8192)
CHUNKS, CW = 4, 512
HOPS = ((4, 3), (3, 4))

TRANSFERS = dict(wa=(CHUNKS, 4), wz=(2, CHUNKS, 5), ws=(CHUNKS, 9), c1=(4,), c2=(3, 2), t=(3, 2), lx=(4,), ly=(4,), lgx=(4,),
                 lgy=(4,), om=(CHUNKS, 2), o1=(CHUNKS, 2, 2), o2=(CHUNKS, 4), gm=(2,), g=(2, 2), sb=(3,), z=(8,), gy=(4,), gx=(4,))
BUFFERS = dict(
    wg=((4, 512, 2048), BF16),
    tokg=((512, 2048), BF16),
    cotg=((4, 128, 2048), BF16),
    upv=((16, 2048), BF16), dnv=((16, 512), BF16),
    lx=((4, 16, 512), F32), ly=((4, 16, 512), F32), lowv=((16, 512), BF16),
    lgx=((4, 16, 128), F32), lgv=((4, 16, 128), BF16),
    of=((512, 2048), F32), os=((512, 2048), BF16), om=((2, 128, 1024), BF16), orx=((2, 128, 2048), BF16), ob=((128, 2048), BF16),
    gf=((512, 512), F32), gs=((3, 512, 512), BF16), gt=((2, 512, 256), F32), gm=((2, 512, 256), BF16), gr=((2, 512, 512), BF16), tgv=((512, 512), BF16),
    gab=((2, 16, 512), F32), sibin=((16, 512), F32), zin=((8, 16, 512), F32), gav=((2, 16, 512), F32),
)


def dot(a, b, da, db):
    return lax.dot_general(a, b, (((da,), (db,)), ((), ())), preferred_element_type=F32)


def kernel(tok, w, down, up, cot, out, tg, ga, gb, *scratch):
    (wg, tokg, cotg, upv, dnv, lx, ly, lowv, lgx, lgv, of, os, om, orx, ob, gf, gs, gt, gm, gr, tgv, gab, sibin, zin, gav) = scratch[: len(BUFFERS)]
    loc, sems = scratch[len(BUFFERS)], scratch[len(BUFFERS) + 1 :]
    sems = {name: sems[2 * i : 2 * i + 2] for i, name in enumerate(TRANSFERS)}
    dp, t = lax.axis_index("dp"), lax.axis_index("tensor")
    z, c = lax.div(dp, 2), lax.rem(dp, 2)
    y, x = lax.div(t, 4), lax.rem(t, 4)

    def row(d):
        return (dp, y * 4 + lax.rem(x + d, 4))

    def col(d):
        return (dp, lax.rem(y + d, 4) * 4 + x)

    def zed(d):
        return (lax.rem(z + d, 8) * 2 + c, t)

    sib = (z * 2 + 1 - c, t)
    sends, pending, locals_ = [], {}, []

    def remote(name, idx, src, dst, dev):
        send, recv = sems[name]
        return pltpu.make_async_remote_copy(src, dst, send.at[idx], recv.at[idx], device_id=dev, device_id_type=MESH)

    def push(name, idx, src, dst, dev):
        cp = remote(name, idx, src, dst, dev)
        cp.start()
        sends.append(cp)
        pending[name, idx] = cp

    def arrive(name, idx, dst=None):
        cp = pending.pop((name, idx))
        (cp if dst is None else remote(name, idx, dst, dst, sib)).wait_recv()

    def local(src, dst):
        cp = pltpu.make_async_copy(src, dst, loc.at[len(locals_)])
        cp.start()
        locals_.append(cp)
        return cp

    def slab(i, size):
        return pl.ds(pl.multiple_of(i * size, size), size)

    ld_w = local(w.at[:, slab(x, 2048)], wg.at[0])
    ld_tok = local(tok, tokg.at[:, pl.ds(0, 512)])
    ld_dn = local(down, dnv)
    ld_up = local(up.at[:, slab(x, 2048)], upv)
    ld_cot = local(cot.at[:, slab(x, 2048)], cotg.at[0, slab(x, 32), :])

    bar = pltpu.get_barrier_semaphore()
    peers = [row(d) for d in (1, 2, 3)] + [col(d) for d in (1, 2, 3)] + [zed(d) for d in range(1, 8)] + [sib]
    for dev in peers:
        pl.semaphore_signal(bar, inc=1, device_id=dev, device_id_type=MESH)
    pl.semaphore_wait(bar, len(peers))

    for j in range(CHUNKS):
        for d in (2, 1, 3):
            n0 = pl.multiple_of(lax.rem(x + d, 4) * 2048 + j * CW, CW)
            push("wa", (j, d), w.at[slab(dp, 32), pl.ds(n0, CW)], wg.at[4 - d, slab(dp, 32), pl.ds(j * CW, CW)], row(d))
    for d in (2, 1, 3):
        push("c1", (d,), cot.at[:, slab(lax.rem(x + d, 4), 2048)], cotg.at[0, slab(x, 32), :], row(d))

    ld_tok.wait()
    ld_dn.wait()
    lx[0] = dot(dnv[...], tokg[:, pl.ds(0, 512)], 1, 1)
    for d in (1, 2, 3):
        push("lx", (d,), lx.at[0], lx.at[4 - d], row(d))

    def half(ref, r, h):
        return ref.at[r, pl.ds(h * 64, 64), :] if ref is cotg else ref.at[pl.ds(h * 256, 256), pl.ds(r * 512, 512)]

    def spread(name, ref, to):
        for i in (0, 1):
            push(name, (0, i), half(ref, 0, i), half(ref, 3, i), to(1))
            push(name, (1, i), half(ref, 0, 1 - i), half(ref, 1, 1 - i), to(3))

    def spread_on(name, ref, to):
        arrive(name, (0, 0))
        push(name, (2, 0), half(ref, 3, 0), half(ref, 2, 0), to(1))
        arrive(name, (1, 0))
        push(name, (2, 1), half(ref, 1, 1), half(ref, 2, 1), to(3))

    def spread_end(name):
        for idx in ((0, 1), (1, 1), (2, 0), (2, 1)):
            arrive(name, idx)

    spread("t", tokg, row)

    def part(zz, cc, j):
        return wg.at[pl.ds(1, 3), slab(zz * 2 + cc, 32), pl.ds(j * CW, CW)]

    def origin(k, s):
        return lax.rem(z + (8 - s if k == 0 else s), 8)

    def to_sib(zz, j, i):
        push("ws", (j, i), part(zz, c, j), part(zz, c, j), sib)

    def send_z(zz, j, k, s):
        push("wz", (k, j, s), part(zz, c, j), part(zz, c, j), zed(1 if k == 0 else 7))

    def step_z(s, j):
        for k in (0, 1):
            if s <= HOPS[j % 2][k]:
                zz = origin(k, s)
                arrive("wz", (k, j, s), part(zz, c, j))
                if s < HOPS[j % 2][k]:
                    send_z(zz, j, k, s + 1)
                to_sib(zz, j, s if k == 0 else 4 + s)

    for j in range(CHUNKS):
        for d in (1, 2, 3):
            arrive("wa", (j, d))
        send_z(z, j, 0, 1)
        send_z(z, j, 1, 1)
        to_sib(z, j, 0)
    step_z(1, 0)
    step_z(1, 1)

    ld_up.wait()
    ld_cot.wait()
    for d in (1, 2, 3):
        arrive("c1", (d,), cotg.at[0, slab(lax.rem(x + 4 - d, 4), 32), :])
    lgx[0] = dot(upv[...], cotg[0], 1, 1)
    for d in (1, 2, 3):
        push("lgx", (d,), lgx.at[0], lgx.at[4 - d], row(d))
    for d in (1, 2, 3):
        arrive("lx", (d,))
    ly[0] = (lx[0] + lx[1]) + (lx[2] + lx[3])
    for d in (1, 2, 3):
        push("ly", (d,), ly.at[0], ly.at[4 - d], col(d))
    spread("c2", cotg, col)
    step_z(1, 2)
    step_z(1, 3)
    for j in range(CHUNKS):
        step_z(2, j)
    spread_on("t", tokg, row)
    spread_on("c2", cotg, col)
    for d in (1, 2, 3):
        arrive("lgx", (d,))
    lgv[0] = ((lgx[0] + lgx[1]) + (lgx[2] + lgx[3])).astype(BF16)
    for d in (1, 2, 3):
        push("lgy", (d,), lgv.at[0], lgv.at[4 - d], col(d))
    for j in range(CHUNKS):
        step_z(3, j)

    for d in (1, 2, 3):
        arrive("ly", (d,))
        arrive("lgy", (d,))
    lowv[...] = ((ly[0] + ly[1]) + (ly[2] + ly[3])).astype(BF16)
    spread_end("c2")
    parts_a = [dot(lgv[r], tokg[slab(lax.rem(y + r, 4), 128), pl.ds(0, 512)], 1, 0) for r in range(4)]
    gab[0] = (parts_a[0] + parts_a[1]) + (parts_a[2] + parts_a[3])
    parts_b = [dot(lowv[:, slab(lax.rem(y + r, 4), 128)], cotg[r, :, slab(y, 512)], 1, 0) for r in range(4)]
    gab[1] = (parts_b[0] + parts_b[1]) + (parts_b[2] + parts_b[3])
    push("sb", (0,), gab.at[1 - c], sibin, sib)

    for j in range(CHUNKS):
        step_z(4, j)

    def weight(j):
        arrive("ws", (j, 0), part(z, 1 - c, j))
        for k in (0, 1):
            for s in range(1, HOPS[j % 2][k] + 1):
                arrive("ws", (j, s if k == 0 else 4 + s), part(origin(k, s), 1 - c, j))

    up1, up2, up3 = (slab(lax.rem(y + d, 4), 128) for d in (1, 2, 3))

    def forward(j):
        @pl.loop(0, 2)
        def _(q):
            cols = slab(j * 2 + q, 256)
            acc = dot(tokg[...], wg[:, :, cols].reshape(2048, 256), 1, 0)
            of[:, cols] = acc
            os[:, cols] = acc.astype(BF16)

        lo, hi, mid = pl.ds(j * CW, 256), pl.ds(j * CW + 256, 256), pl.ds(j * 256, 256)
        push("om", (j, 0), os.at[up2, lo], om.at[0, :, mid], col(1))
        push("om", (j, 1), os.at[up2, hi], om.at[1, :, mid], col(3))
        push("o1", (j, 0, 1), os.at[up1, hi], orx.at[0, :, hi], col(1))
        push("o1", (j, 1, 0), os.at[up3, lo], orx.at[1, :, lo], col(3))

    def forward_on(j):
        lo, hi, mid = pl.ds(j * CW, 256), pl.ds(j * CW + 256, 256), pl.ds(j * 256, 256)
        arrive("om", (j, 0))
        os[up1, lo] = (of[up1, lo] + om[0, :, mid].astype(F32)).astype(BF16)
        push("o1", (j, 0, 0), os.at[up1, lo], orx.at[0, :, lo], col(1))
        arrive("om", (j, 1))
        os[up3, hi] = (of[up3, hi] + om[1, :, mid].astype(F32)).astype(BF16)
        push("o1", (j, 1, 1), os.at[up3, hi], orx.at[1, :, hi], col(3))

    def backward(r):
        for h in (1, 0) if r == 1 else (0, 1):
            cols = pl.ds(h * 256, 256)
            acc = dot(cotg[...].reshape(512, 2048), wg[r, cols, :], 1, 1)
            if r == 0:
                gf[:, cols] = acc
            elif r == 2:
                gs[1, :, cols] = acc.astype(BF16)
                push("gm", (h,), gs.at[1, :, cols], gm.at[h], row(1 if h == 0 else 3))
            elif (r, h) in ((1, 0), (3, 1)):
                gt[h] = acc
            else:
                gs[r - 1, :, cols] = acc.astype(BF16)
                push("g", (1 - h, h), gs.at[r - 1, :, cols], gr.at[1 - h, :, cols], row(r))

    def backward_on(h):
        cols = pl.ds(h * 256, 256)
        arrive("gm", (h,))
        gs[2 * h, :, cols] = (gt[h] + gm[h].astype(F32)).astype(BF16)
        push("g", (h, h), gs.at[2 * h, :, cols], gr.at[h, :, cols], row(1 if h == 0 else 3))

    eight = slab(c, 8)

    def block(yy):
        return gb.at[eight, pl.ds(pl.multiple_of(x * 2048 + yy * 512, 512), 512)]

    arrive("sb", (0,))
    zin[z] = gab[c] + sibin[...]
    for d in range(1, 8):
        push("z", (d,), zin.at[z], zin.at[z], zed(d))
    ld_w.wait()
    for j in range(CHUNKS):
        weight(j)
    backward(2)
    spread_end("t")
    forward(0)
    backward(1)
    backward(3)
    forward(1)
    backward_on(0)
    backward_on(1)
    forward_on(0)
    for d in range(1, 8):
        arrive("z", (d,), zin.at[lax.rem(z + 8 - d, 8)])
    total = zin[0]
    for i in range(1, 8):
        total = total + zin[i]
    gav[c] = total * FACTOR
    push("sb", (1,), gav.at[c], gav.at[c], sib)
    forward(2)
    arrive("sb", (1,), gav.at[1 - c])
    ga_out = local(gav.at[0], ga)
    for d in (1, 2, 3):
        push("gy", (d,), gav.at[1, eight, :], block(y), col(d))
    gb_own = local(gav.at[1, eight, :], block(y))
    forward_on(1)
    forward(3)
    forward_on(2)
    backward(0)
    forward_on(3)

    def output(j):
        cols = pl.ds(j * CW, CW)
        for k in (0, 1):
            for h in (0, 1):
                arrive("o1", (j, k, h))
        acc = of[slab(y, 128), cols] + orx[0, :, cols].astype(F32) + orx[1, :, cols].astype(F32)
        acc += SCALE * dot(lowv[:, slab(y, 128)], upv[:, cols], 0, 0)
        ob[:, cols] = acc.astype(BF16)
        here = pl.ds(pl.multiple_of(x * 2048 + j * CW, CW), CW)
        for d in (2, 1, 3):
            push("o2", (j, d), ob.at[slab(lax.rem(x + d, 4), 32), cols], out.at[:, here], row(d))
        return local(ob.at[slab(x, 32), cols], out.at[:, here])

    gb_own.wait()
    for d in (1, 2, 3):
        arrive("gy", (d,), block(lax.rem(y + 4 - d, 4)))
    for d in (1, 2, 3):
        push("gx", (d,), gb.at[eight, slab(x, 2048)], gb.at[eight, slab(x, 2048)], row(d))
    own = [output(0), output(1), output(2)]
    for d in (1, 2, 3):
        arrive("gx", (d,), gb.at[eight, slab(lax.rem(x + 4 - d, 4), 2048)])
    push("sb", (2,), gb.at[eight, :], gb.at[eight, :], sib)
    own.append(output(3))

    for h in range(2):
        cols = pl.ds(h * 256, 256)
        arrive("g", (0, h))
        arrive("g", (1, h))
        for q in range(4):
            rows = pl.ds(q * 128, 128)
            acc = gf[rows, cols] + gr[0, rows, cols].astype(F32) + gr[1, rows, cols].astype(F32)
            acc += SCALE * dot(lgv[q], dnv[:, cols], 0, 0)
            tgv[slab(lax.rem(y + q, 4), 128), cols] = acc.astype(BF16)
    tg_out = local(tgv, tg)

    arrive("sb", (2,), gb.at[slab(1 - c, 8), :])
    for j in range(CHUNKS):
        own[j].wait()
        for d in (1, 2, 3):
            there = pl.ds(pl.multiple_of(lax.rem(x + 4 - d, 4) * 2048 + j * CW, CW), CW)
            arrive("o2", (j, d), out.at[:, there])
    tg_out.wait()
    ga_out.wait()
    for cp in sends:
        cp.wait_send()


def finish(a, b, c, d, oa, ob, oc, od, va, vb, vc, vd, sem):
    loads = [pltpu.make_async_copy(s, v, sem.at[0, i]) for i, (s, v) in enumerate(((a, va), (b, vb), (c, vc), (d, vd)))]
    stores = [pltpu.make_async_copy(v, o, sem.at[1, i]) for i, (v, o) in enumerate(((va, oa), (vb, ob), (vc, oc), (vd, od)))]
    for cp in loads:
        cp.start()
    for load, store in zip(loads, stores):
        load.wait()
        store.start()
    for cp in stores:
        cp.wait()


def per_device(tokens, weight, down_adapter, up_adapter, cotangent):
    dma = pltpu.SemaphoreType.DMA
    any_ = pl.BlockSpec(memory_space=pl.ANY)
    results = (
        jax.ShapeDtypeStruct((32, 8192), BF16),
        jax.ShapeDtypeStruct((512, 512), BF16),
        jax.ShapeDtypeStruct((16, 512), F32),
        jax.ShapeDtypeStruct((16, 8192), F32),
    )
    made = pl.pallas_call(
        kernel,
        out_shape=results,
        in_specs=[any_] * 5,
        out_specs=(any_,) * 4,
        scratch_shapes=[pltpu.VMEM(*b) for b in BUFFERS.values()]
        + [dma((16,))]
        + [dma(shape) for shape in TRANSFERS.values() for _ in range(2)],
        compiler_params=pltpu.CompilerParams(collective_id=0, has_side_effects=True, vmem_limit_bytes=56 * 2**20),
        name="projection",
    )(tokens, weight, down_adapter.T, up_adapter, cotangent)
    output, token_gradient, grad_a, grad_b = pl.pallas_call(
        finish,
        out_shape=results,
        in_specs=[any_] * 4,
        out_specs=(any_,) * 4,
        scratch_shapes=[pltpu.VMEM(r.shape, r.dtype) for r in results] + [dma((2, 4))],
        name="results",
    )(*made)
    return output, token_gradient, grad_a.T, grad_b


def solution(mesh):
    placed = (
        P("dp", "tensor"),
        P("tensor", None),
        P("tensor", None),
        P(),
        P(("dp", "tensor"), None),
    )
    return jax.shard_map(
        per_device,
        mesh=mesh,
        in_specs=placed,
        out_specs=(P(("dp", "tensor"), None), P("dp", "tensor"), P("tensor", None), P()),
        check_vma=False,
    )
```

```python
import math

import jax
import jax.numpy as jnp
from jax import lax
from jax.experimental import pallas as pl
from jax.experimental.pallas import tpu as pltpu
from jax.sharding import PartitionSpec as P

MESH = pl.DeviceIdType.MESH
F32, BF16 = jnp.float32, jnp.bfloat16
SCALE = 0.5
FACTOR = SCALE / math.sqrt(8192)
CHUNKS, CW = 4, 512
UNITS = ((2, 0), (2, 1), (1, 0), (3, 0), (1, 1), (3, 1))
HOPS = ((4, 3), (3, 4))

TRANSFERS = dict(wa=(6,), wz=(2, 6, 5), ws=(6, 9), c1=(4,), c2=(3, 2), t=(3, 2), lx=(4,), ly=(4,), lgx=(4,),
                 lgy=(4,), om=(CHUNKS, 2), o1=(CHUNKS, 2, 2), o2=(CHUNKS, 4), gm=(2,), g=(2, 2), sb=(3,), z=(8,), gy=(4,), gx=(4,))
BUFFERS = dict(
    wg=((4, 512, 2048), BF16),
    tokg=((512, 2048), BF16),
    cotg=((4, 128, 2048), BF16),
    upv=((16, 2048), BF16), dnv=((16, 512), BF16),
    lx=((4, 16, 512), F32), ly=((4, 16, 512), F32), lowv=((16, 512), BF16),
    lgx=((4, 16, 128), F32), lgv=((4, 16, 128), BF16),
    of=((512, 2048), F32), os=((512, 2048), BF16), om=((2, 128, 1024), BF16), orx=((2, 128, 2048), BF16), ob=((128, 2048), BF16),
    gf=((512, 512), F32), gs=((3, 512, 512), BF16), gt=((2, 512, 256), F32), gm=((2, 512, 256), BF16), gr=((2, 512, 512), BF16), tgv=((512, 512), BF16),
    gab=((2, 16, 512), F32), sibin=((16, 512), F32), zin=((8, 16, 512), F32), gav=((2, 16, 512), F32),
)


def dot(a, b, da, db):
    return lax.dot_general(a, b, (((da,), (db,)), ((), ())), preferred_element_type=F32)


def kernel(tok, w, down, up, cot, out, tg, ga, gb, *scratch):
    (wg, tokg, cotg, upv, dnv, lx, ly, lowv, lgx, lgv, of, os, om, orx, ob, gf, gs, gt, gm, gr, tgv, gab, sibin, zin, gav) = scratch[: len(BUFFERS)]
    loc, sems = scratch[len(BUFFERS)], scratch[len(BUFFERS) + 1 :]
    sems = {name: sems[2 * i : 2 * i + 2] for i, name in enumerate(TRANSFERS)}
    dp, t = lax.axis_index("dp"), lax.axis_index("tensor")
    z, c = lax.div(dp, 2), lax.rem(dp, 2)
    y, x = lax.div(t, 4), lax.rem(t, 4)

    def row(d):
        return (dp, y * 4 + lax.rem(x + d, 4))

    def col(d):
        return (dp, lax.rem(y + d, 4) * 4 + x)

    def zed(d):
        return (lax.rem(z + d, 8) * 2 + c, t)

    sib = (z * 2 + 1 - c, t)
    sends, pending, locals_ = [], {}, []

    def remote(name, idx, src, dst, dev):
        send, recv = sems[name]
        return pltpu.make_async_remote_copy(src, dst, send.at[idx], recv.at[idx], device_id=dev, device_id_type=MESH)

    def push(name, idx, src, dst, dev):
        cp = remote(name, idx, src, dst, dev)
        cp.start()
        sends.append(cp)
        pending[name, idx] = cp

    def arrive(name, idx, dst=None):
        cp = pending.pop((name, idx))
        (cp if dst is None else remote(name, idx, dst, dst, sib)).wait_recv()

    def local(src, dst):
        cp = pltpu.make_async_copy(src, dst, loc.at[len(locals_)])
        cp.start()
        locals_.append(cp)
        return cp

    def slab(i, size):
        return pl.ds(pl.multiple_of(i * size, size), size)

    ld_w = local(w.at[:, slab(x, 2048)], wg.at[0])
    ld_tok = local(tok, tokg.at[:, pl.ds(0, 512)])
    ld_dn = local(down, dnv)
    ld_up = local(up.at[:, slab(x, 2048)], upv)
    ld_cot = local(cot.at[:, slab(x, 2048)], cotg.at[0, slab(x, 32), :])

    bar = pltpu.get_barrier_semaphore()
    peers = [row(d) for d in (1, 2, 3)] + [col(d) for d in (1, 2, 3)] + [zed(d) for d in range(1, 8)] + [sib]
    for dev in peers:
        pl.semaphore_signal(bar, inc=1, device_id=dev, device_id_type=MESH)
    pl.semaphore_wait(bar, len(peers))

    def send_w(u):
        r, h = UNITS[u]
        n0 = pl.multiple_of(lax.rem(x + 4 - r, 4) * 2048 + h * 1024, 1024)
        push("wa", (u,), w.at[slab(dp, 32), pl.ds(n0, 1024)], wg.at[r, slab(dp, 32), pl.ds(h * 1024, 1024)], row(4 - r))

    send_w(0)
    send_w(1)
    for d in (2, 1, 3):
        push("c1", (d,), cot.at[:, slab(lax.rem(x + d, 4), 2048)], cotg.at[0, slab(x, 32), :], row(d))
    for u in range(2, 6):
        send_w(u)

    def part(zz, cc, u):
        r, h = UNITS[u]
        return wg.at[r, slab(zz * 2 + cc, 32), pl.ds(h * 1024, 1024)]

    def origin(k, s):
        return lax.rem(z + (8 - s if k == 0 else s), 8)

    def to_sib(zz, u, i):
        push("ws", (u, i), part(zz, c, u), part(zz, c, u), sib)

    def send_z(zz, u, k, s):
        push("wz", (k, u, s), part(zz, c, u), part(zz, c, u), zed(1 if k == 0 else 7))

    def start_z(u):
        arrive("wa", (u,))
        send_z(z, u, 0, 1)
        send_z(z, u, 1, 1)
        to_sib(z, u, 0)

    def step_z(s, u):
        hops = HOPS[u % 2]
        for k in (0, 1):
            if s <= hops[k]:
                zz = origin(k, s)
                arrive("wz", (k, u, s), part(zz, c, u))
                if s < hops[k]:
                    send_z(zz, u, k, s + 1)
                to_sib(zz, u, s if k == 0 else 4 + s)

    def weight(*units):
        for u in units:
            arrive("ws", (u, 0), part(z, 1 - c, u))
            for k in (0, 1):
                for s in range(1, HOPS[u % 2][k] + 1):
                    arrive("ws", (u, s if k == 0 else 4 + s), part(origin(k, s), 1 - c, u))

    def half(ref, r, h):
        return ref.at[r, pl.ds(h * 64, 64), :] if ref is cotg else ref.at[pl.ds(h * 256, 256), pl.ds(r * 512, 512)]

    def spread(name, ref, to):
        for i in (0, 1):
            push(name, (0, i), half(ref, 0, i), half(ref, 3, i), to(1))
            push(name, (1, i), half(ref, 0, 1 - i), half(ref, 1, 1 - i), to(3))

    def spread_on(name, ref, to):
        arrive(name, (0, 0))
        push(name, (2, 0), half(ref, 3, 0), half(ref, 2, 0), to(1))
        arrive(name, (1, 0))
        push(name, (2, 1), half(ref, 1, 1), half(ref, 2, 1), to(3))

    def spread_end(name):
        for idx in ((0, 1), (1, 1), (2, 0), (2, 1)):
            arrive(name, idx)

    start_z(0)
    start_z(1)
    ld_tok.wait()
    ld_dn.wait()
    lx[0] = dot(dnv[...], tokg[:, pl.ds(0, 512)], 1, 1)
    for d in (1, 2, 3):
        push("lx", (d,), lx.at[0], lx.at[4 - d], row(d))
    step_z(1, 0)
    step_z(1, 1)
    ld_up.wait()
    ld_cot.wait()
    for d in (1, 2, 3):
        arrive("c1", (d,), cotg.at[0, slab(lax.rem(x + 4 - d, 4), 32), :])
    spread("c2", cotg, col)
    lgx[0] = dot(upv[...], cotg[0], 1, 1)
    for d in (1, 2, 3):
        push("lgx", (d,), lgx.at[0], lgx.at[4 - d], row(d))
    spread("t", tokg, row)
    start_z(2)
    start_z(3)
    step_z(2, 0)
    step_z(2, 1)
    start_z(4)
    start_z(5)
    for d in (1, 2, 3):
        arrive("lx", (d,))
    ly[0] = (lx[0] + lx[1]) + (lx[2] + lx[3])
    for d in (1, 2, 3):
        push("ly", (d,), ly.at[0], ly.at[4 - d], col(d))
    step_z(1, 2)
    step_z(1, 3)
    step_z(3, 0)
    step_z(3, 1)
    step_z(1, 4)
    step_z(1, 5)
    spread_on("c2", cotg, col)
    spread_on("t", tokg, row)
    for d in (1, 2, 3):
        arrive("lgx", (d,))
    lgv[0] = ((lgx[0] + lgx[1]) + (lgx[2] + lgx[3])).astype(BF16)
    for d in (1, 2, 3):
        push("lgy", (d,), lgv.at[0], lgv.at[4 - d], col(d))
    step_z(4, 0)
    step_z(4, 1)
    for u in range(2, 6):
        step_z(2, u)
    step_z(3, 2)
    step_z(3, 3)

    up1, up2, up3 = (slab(lax.rem(y + d, 4), 128) for d in (1, 2, 3))

    def forward(j):
        @pl.loop(0, 2)
        def _(q):
            cols = slab(j * 2 + q, 256)
            acc = dot(tokg[...], wg[:, :, cols].reshape(2048, 256), 1, 0)
            of[:, cols] = acc
            os[:, cols] = acc.astype(BF16)

        lo, hi, mid = pl.ds(j * CW, 256), pl.ds(j * CW + 256, 256), pl.ds(j * 256, 256)
        push("om", (j, 0), os.at[up2, lo], om.at[0, :, mid], col(1))
        push("om", (j, 1), os.at[up2, hi], om.at[1, :, mid], col(3))
        push("o1", (j, 0, 1), os.at[up1, hi], orx.at[0, :, hi], col(1))
        push("o1", (j, 1, 0), os.at[up3, lo], orx.at[1, :, lo], col(3))

    def forward_on(j):
        lo, hi, mid = pl.ds(j * CW, 256), pl.ds(j * CW + 256, 256), pl.ds(j * 256, 256)
        arrive("om", (j, 0))
        os[up1, lo] = (of[up1, lo] + om[0, :, mid].astype(F32)).astype(BF16)
        push("o1", (j, 0, 0), os.at[up1, lo], orx.at[0, :, lo], col(1))
        arrive("om", (j, 1))
        os[up3, hi] = (of[up3, hi] + om[1, :, mid].astype(F32)).astype(BF16)
        push("o1", (j, 1, 1), os.at[up3, hi], orx.at[1, :, hi], col(3))

    def backward(r):
        for h in (1, 0) if r == 1 else (0, 1):
            cols = pl.ds(h * 256, 256)
            acc = dot(cotg[...].reshape(512, 2048), wg[r, cols, :], 1, 1)
            if r == 0:
                gf[:, cols] = acc
            elif r == 2:
                gs[1, :, cols] = acc.astype(BF16)
                push("gm", (h,), gs.at[1, :, cols], gm.at[h], row(1 if h == 0 else 3))
            elif (r, h) in ((1, 0), (3, 1)):
                gt[h] = acc
            else:
                gs[r - 1, :, cols] = acc.astype(BF16)
                push("g", (1 - h, h), gs.at[r - 1, :, cols], gr.at[1 - h, :, cols], row(r))

    def backward_on(h):
        cols = pl.ds(h * 256, 256)
        arrive("gm", (h,))
        gs[2 * h, :, cols] = (gt[h] + gm[h].astype(F32)).astype(BF16)
        push("g", (h, h), gs.at[2 * h, :, cols], gr.at[h, :, cols], row(1 if h == 0 else 3))

    eight = slab(c, 8)

    def block(yy):
        return gb.at[eight, pl.ds(pl.multiple_of(x * 2048 + yy * 512, 512), 512)]

    def output(j):
        cols = pl.ds(j * CW, CW)
        for k in (0, 1):
            for h in (0, 1):
                arrive("o1", (j, k, h))
        acc = of[slab(y, 128), cols] + orx[0, :, cols].astype(F32) + orx[1, :, cols].astype(F32)
        acc += SCALE * dot(lowv[:, slab(y, 128)], upv[:, cols], 0, 0)
        ob[:, cols] = acc.astype(BF16)
        here = pl.ds(pl.multiple_of(x * 2048 + j * CW, CW), CW)
        for d in (2, 1, 3):
            push("o2", (j, d), ob.at[slab(lax.rem(x + d, 4), 32), cols], out.at[:, here], row(d))
        return local(ob.at[slab(x, 32), cols], out.at[:, here])

    ld_w.wait()
    spread_end("c2")
    weight(0, 1)
    backward(2)
    step_z(3, 4)
    step_z(3, 5)

    for d in (1, 2, 3):
        arrive("ly", (d,))
        arrive("lgy", (d,))
    lowv[...] = ((ly[0] + ly[1]) + (ly[2] + ly[3])).astype(BF16)
    parts_a = [dot(lgv[r], tokg[slab(lax.rem(y + r, 4), 128), pl.ds(0, 512)], 1, 0) for r in range(4)]
    gab[0] = (parts_a[0] + parts_a[1]) + (parts_a[2] + parts_a[3])
    parts_b = [dot(lowv[:, slab(lax.rem(y + r, 4), 128)], cotg[r, :, slab(y, 512)], 1, 0) for r in range(4)]
    gab[1] = (parts_b[0] + parts_b[1]) + (parts_b[2] + parts_b[3])
    push("sb", (0,), gab.at[1 - c], sibin, sib)
    step_z(4, 2)
    step_z(4, 3)
    spread_end("t")
    weight(2, 3)
    forward(0)
    step_z(4, 4)
    step_z(4, 5)
    arrive("sb", (0,))
    zin[z] = gab[c] + sibin[...]
    for d in range(1, 8):
        push("z", (d,), zin.at[z], zin.at[z], zed(d))
    forward(1)
    forward_on(0)
    weight(4, 5)
    backward(1)
    backward(3)
    forward_on(1)
    forward(2)
    backward_on(0)
    backward_on(1)
    for d in range(1, 8):
        arrive("z", (d,), zin.at[lax.rem(z + 8 - d, 8)])
    total = zin[0]
    for i in range(1, 8):
        total = total + zin[i]
    gav[c] = total * FACTOR
    push("sb", (1,), gav.at[c], gav.at[c], sib)
    own = [output(0)]
    arrive("sb", (1,), gav.at[1 - c])
    ga_out = local(gav.at[0], ga)
    for d in (1, 2, 3):
        push("gy", (d,), gav.at[1, eight, :], block(y), col(d))
    gb_own = local(gav.at[1, eight, :], block(y))
    forward(3)
    forward_on(2)
    own.append(output(1))
    forward_on(3)
    backward(0)
    gb_own.wait()
    for d in (1, 2, 3):
        arrive("gy", (d,), block(lax.rem(y + 4 - d, 4)))
    for d in (1, 2, 3):
        push("gx", (d,), gb.at[eight, slab(x, 2048)], gb.at[eight, slab(x, 2048)], row(d))
    own.append(output(2))
    own.append(output(3))
    for d in (1, 2, 3):
        arrive("gx", (d,), gb.at[eight, slab(lax.rem(x + 4 - d, 4), 2048)])
    push("sb", (2,), gb.at[eight, :], gb.at[eight, :], sib)

    for h in range(2):
        cols = pl.ds(h * 256, 256)
        arrive("g", (0, h))
        arrive("g", (1, h))
        for q in range(4):
            rows = pl.ds(q * 128, 128)
            acc = gf[rows, cols] + gr[0, rows, cols].astype(F32) + gr[1, rows, cols].astype(F32)
            acc += SCALE * dot(lgv[q], dnv[:, cols], 0, 0)
            tgv[slab(lax.rem(y + q, 4), 128), cols] = acc.astype(BF16)
    tg_out = local(tgv, tg)

    arrive("sb", (2,), gb.at[slab(1 - c, 8), :])
    for j in range(CHUNKS):
        own[j].wait()
        for d in (1, 2, 3):
            there = pl.ds(pl.multiple_of(lax.rem(x + 4 - d, 4) * 2048 + j * CW, CW), CW)
            arrive("o2", (j, d), out.at[:, there])
    tg_out.wait()
    ga_out.wait()
    for cp in sends:
        cp.wait_send()


def finish(a, b, c, d, oa, ob, oc, od, va, vb, vc, vd, sem):
    loads = [pltpu.make_async_copy(s, v, sem.at[0, i]) for i, (s, v) in enumerate(((a, va), (b, vb), (c, vc), (d, vd)))]
    stores = [pltpu.make_async_copy(v, o, sem.at[1, i]) for i, (v, o) in enumerate(((va, oa), (vb, ob), (vc, oc), (vd, od)))]
    for cp in loads:
        cp.start()
    for load, store in zip(loads, stores):
        load.wait()
        store.start()
    for cp in stores:
        cp.wait()


def per_device(tokens, weight, down_adapter, up_adapter, cotangent):
    dma = pltpu.SemaphoreType.DMA
    any_ = pl.BlockSpec(memory_space=pl.ANY)
    results = (
        jax.ShapeDtypeStruct((32, 8192), BF16),
        jax.ShapeDtypeStruct((512, 512), BF16),
        jax.ShapeDtypeStruct((16, 512), F32),
        jax.ShapeDtypeStruct((16, 8192), F32),
    )
    made = pl.pallas_call(
        kernel,
        out_shape=results,
        in_specs=[any_] * 5,
        out_specs=(any_,) * 4,
        scratch_shapes=[pltpu.VMEM(*b) for b in BUFFERS.values()]
        + [dma((16,))]
        + [dma(shape) for shape in TRANSFERS.values() for _ in range(2)],
        compiler_params=pltpu.CompilerParams(collective_id=0, has_side_effects=True, vmem_limit_bytes=56 * 2**20),
        name="projection",
    )(tokens, weight, down_adapter.T, up_adapter, cotangent)
    output, token_gradient, grad_a, grad_b = pl.pallas_call(
        finish,
        out_shape=results,
        in_specs=[any_] * 4,
        out_specs=(any_,) * 4,
        scratch_shapes=[pltpu.VMEM(r.shape, r.dtype) for r in results] + [dma((2, 4))],
        name="results",
    )(*made)
    return output, token_gradient, grad_a.T, grad_b


def solution(mesh):
    placed = (
        P("dp", "tensor"),
        P("tensor", None),
        P("tensor", None),
        P(),
        P(("dp", "tensor"), None),
    )
    return jax.shard_map(
        per_device,
        mesh=mesh,
        in_specs=placed,
        out_specs=(P(("dp", "tensor"), None), P("dp", "tensor"), P("tensor", None), P()),
        check_vma=False,
    )
```

```python
import math

import jax
import jax.numpy as jnp
from jax import lax
from jax.experimental import pallas as pl
from jax.experimental.pallas import tpu as pltpu
from jax.sharding import PartitionSpec as P

MESH = pl.DeviceIdType.MESH
F32, BF16 = jnp.float32, jnp.bfloat16
SCALE = 0.5
FACTOR = SCALE / math.sqrt(8192)
CHUNKS, CW = 4, 512
UNITS = ((2, 0), (2, 1), (1, 0), (3, 0), (1, 1), (3, 1))
HOPS = ((4, 3), (3, 4))

TRANSFERS = dict(wa=(6,), wz=(2, 6, 5), ws=(6, 9), c1=(4,), c2=(3, 2), t=(3, 2), lx=(4,), ly=(4,), lgx=(4,),
                 lgy=(4,), om=(CHUNKS, 2), o1=(CHUNKS, 2, 2), o2=(CHUNKS, 4), gm=(2,), g=(2, 2), sb=(3,), z=(8,), gy=(4,), gx=(4,))
BUFFERS = dict(
    wg=((4, 512, 2048), BF16),
    tokg=((512, 2048), BF16),
    cotg=((4, 128, 2048), BF16),
    upv=((16, 2048), BF16), dnv=((16, 512), BF16),
    lx=((4, 16, 512), F32), ly=((4, 16, 512), F32), lowv=((16, 512), BF16),
    lgx=((4, 16, 128), F32), lgv=((4, 16, 128), BF16),
    of=((512, 2048), F32), os=((512, 2048), BF16), om=((2, 128, 1024), BF16), orx=((2, 128, 2048), BF16), ob=((128, 2048), BF16),
    gf=((512, 512), F32), gs=((3, 512, 512), BF16), gt=((2, 512, 256), F32), gm=((2, 512, 256), BF16), gr=((2, 512, 512), BF16), tgv=((512, 512), BF16),
    gab=((2, 16, 512), F32), sibin=((16, 512), F32), zin=((8, 16, 512), F32), gav=((2, 16, 512), F32),
)


def dot(a, b, da, db):
    return lax.dot_general(a, b, (((da,), (db,)), ((), ())), preferred_element_type=F32)


def kernel(tok, w, down, up, cot, out, tg, ga, gb, *scratch):
    (wg, tokg, cotg, upv, dnv, lx, ly, lowv, lgx, lgv, of, os, om, orx, ob, gf, gs, gt, gm, gr, tgv, gab, sibin, zin, gav) = scratch[: len(BUFFERS)]
    loc, sems = scratch[len(BUFFERS)], scratch[len(BUFFERS) + 1 :]
    sems = {name: sems[2 * i : 2 * i + 2] for i, name in enumerate(TRANSFERS)}
    dp, t = lax.axis_index("dp"), lax.axis_index("tensor")
    z, c = lax.div(dp, 2), lax.rem(dp, 2)
    y, x = lax.div(t, 4), lax.rem(t, 4)

    def row(d):
        return (dp, y * 4 + lax.rem(x + d, 4))

    def col(d):
        return (dp, lax.rem(y + d, 4) * 4 + x)

    def zed(d):
        return (lax.rem(z + d, 8) * 2 + c, t)

    sib = (z * 2 + 1 - c, t)
    sends, pending, locals_ = [], {}, []

    def remote(name, idx, src, dst, dev):
        send, recv = sems[name]
        return pltpu.make_async_remote_copy(src, dst, send.at[idx], recv.at[idx], device_id=dev, device_id_type=MESH)

    def push(name, idx, src, dst, dev):
        cp = remote(name, idx, src, dst, dev)
        cp.start()
        sends.append(cp)
        pending[name, idx] = cp

    def arrive(name, idx, dst=None):
        cp = pending.pop((name, idx))
        (cp if dst is None else remote(name, idx, dst, dst, sib)).wait_recv()

    def local(src, dst):
        cp = pltpu.make_async_copy(src, dst, loc.at[len(locals_)])
        cp.start()
        locals_.append(cp)
        return cp

    def slab(i, size):
        return pl.ds(pl.multiple_of(i * size, size), size)

    ld_w = local(w.at[:, slab(x, 2048)], wg.at[0])
    ld_tok = local(tok, tokg.at[:, pl.ds(0, 512)])
    ld_dn = local(down, dnv)
    ld_up = local(up.at[:, slab(x, 2048)], upv)
    ld_cot = local(cot.at[:, slab(x, 2048)], cotg.at[0, slab(x, 32), :])

    bar = pltpu.get_barrier_semaphore()
    peers = [row(d) for d in (1, 2, 3)] + [col(d) for d in (1, 2, 3)] + [zed(d) for d in range(1, 8)] + [sib]
    for dev in peers:
        pl.semaphore_signal(bar, inc=1, device_id=dev, device_id_type=MESH)
    pl.semaphore_wait(bar, len(peers))

    def send_w(u):
        r, h = UNITS[u]
        n0 = pl.multiple_of(lax.rem(x + 4 - r, 4) * 2048 + h * 1024, 1024)
        push("wa", (u,), w.at[slab(dp, 32), pl.ds(n0, 1024)], wg.at[r, slab(dp, 32), pl.ds(h * 1024, 1024)], row(4 - r))

    send_w(0)
    send_w(1)
    for d in (2, 1, 3):
        push("c1", (d,), cot.at[:, slab(lax.rem(x + d, 4), 2048)], cotg.at[0, slab(x, 32), :], row(d))
    for u in range(2, 6):
        send_w(u)

    def part(zz, cc, u):
        r, h = UNITS[u]
        return wg.at[r, slab(zz * 2 + cc, 32), pl.ds(h * 1024, 1024)]

    def origin(k, s):
        return lax.rem(z + (8 - s if k == 0 else s), 8)

    def to_sib(zz, u, i):
        push("ws", (u, i), part(zz, c, u), part(zz, c, u), sib)

    def send_z(zz, u, k, s):
        push("wz", (k, u, s), part(zz, c, u), part(zz, c, u), zed(1 if k == 0 else 7))

    def start_z(u):
        arrive("wa", (u,))
        send_z(z, u, 0, 1)
        send_z(z, u, 1, 1)
        to_sib(z, u, 0)

    def step_z(s, u):
        hops = HOPS[u % 2]
        for k in (0, 1):
            if s <= hops[k]:
                zz = origin(k, s)
                arrive("wz", (k, u, s), part(zz, c, u))
                if s < hops[k]:
                    send_z(zz, u, k, s + 1)
                to_sib(zz, u, s if k == 0 else 4 + s)

    def weight(*units):
        for u in units:
            arrive("ws", (u, 0), part(z, 1 - c, u))
            for k in (0, 1):
                for s in range(1, HOPS[u % 2][k] + 1):
                    arrive("ws", (u, s if k == 0 else 4 + s), part(origin(k, s), 1 - c, u))

    def half(ref, r, h):
        return ref.at[r, pl.ds(h * 64, 64), :] if ref is cotg else ref.at[pl.ds(h * 256, 256), pl.ds(r * 512, 512)]

    def spread(name, ref, to):
        for i in (0, 1):
            push(name, (0, i), half(ref, 0, i), half(ref, 3, i), to(1))
            push(name, (1, i), half(ref, 0, 1 - i), half(ref, 1, 1 - i), to(3))

    def spread_on(name, ref, to):
        arrive(name, (0, 0))
        push(name, (2, 0), half(ref, 3, 0), half(ref, 2, 0), to(1))
        arrive(name, (1, 0))
        push(name, (2, 1), half(ref, 1, 1), half(ref, 2, 1), to(3))

    def spread_end(name):
        for idx in ((0, 1), (1, 1), (2, 0), (2, 1)):
            arrive(name, idx)

    start_z(0)
    start_z(1)
    ld_tok.wait()
    ld_dn.wait()
    lx[0] = dot(dnv[...], tokg[:, pl.ds(0, 512)], 1, 1)
    for d in (1, 2, 3):
        push("lx", (d,), lx.at[0], lx.at[4 - d], row(d))
    step_z(1, 0)
    step_z(1, 1)
    ld_up.wait()
    ld_cot.wait()
    for d in (1, 2, 3):
        arrive("c1", (d,), cotg.at[0, slab(lax.rem(x + 4 - d, 4), 32), :])
    spread("c2", cotg, col)
    lgx[0] = dot(upv[...], cotg[0], 1, 1)
    for d in (1, 2, 3):
        push("lgx", (d,), lgx.at[0], lgx.at[4 - d], row(d))
    spread("t", tokg, row)
    start_z(2)
    start_z(3)
    step_z(2, 0)
    step_z(2, 1)
    start_z(4)
    start_z(5)
    for d in (1, 2, 3):
        arrive("lx", (d,))
    ly[0] = (lx[0] + lx[1]) + (lx[2] + lx[3])
    for d in (1, 2, 3):
        push("ly", (d,), ly.at[0], ly.at[4 - d], col(d))
    step_z(1, 2)
    step_z(1, 3)
    step_z(3, 0)
    step_z(3, 1)
    step_z(1, 4)
    step_z(1, 5)
    spread_on("c2", cotg, col)
    spread_on("t", tokg, row)
    for d in (1, 2, 3):
        arrive("lgx", (d,))
    lgv[0] = ((lgx[0] + lgx[1]) + (lgx[2] + lgx[3])).astype(BF16)
    for d in (1, 2, 3):
        push("lgy", (d,), lgv.at[0], lgv.at[4 - d], col(d))
    step_z(4, 0)
    step_z(4, 1)
    for u in range(2, 6):
        step_z(2, u)
    step_z(3, 2)
    step_z(3, 3)

    up1, up2, up3 = (slab(lax.rem(y + d, 4), 128) for d in (1, 2, 3))

    def forward(j):
        lo, hi, mid = pl.ds(j * CW, 256), pl.ds(j * CW + 256, 256), pl.ds(j * 256, 256)
        for cols in (lo, hi):
            acc = dot(tokg[...], wg[:, :, cols].reshape(2048, 256), 1, 0)
            of[:, cols] = acc
            os[:, cols] = acc.astype(BF16)
            if cols is lo:
                push("om", (j, 0), os.at[up2, lo], om.at[0, :, mid], col(1))
                push("o1", (j, 1, 0), os.at[up3, lo], orx.at[1, :, lo], col(3))
            else:
                push("om", (j, 1), os.at[up2, hi], om.at[1, :, mid], col(3))
                push("o1", (j, 0, 1), os.at[up1, hi], orx.at[0, :, hi], col(1))

    def forward_on(j):
        lo, hi, mid = pl.ds(j * CW, 256), pl.ds(j * CW + 256, 256), pl.ds(j * 256, 256)
        arrive("om", (j, 0))
        os[up1, lo] = (of[up1, lo] + om[0, :, mid].astype(F32)).astype(BF16)
        push("o1", (j, 0, 0), os.at[up1, lo], orx.at[0, :, lo], col(1))
        arrive("om", (j, 1))
        os[up3, hi] = (of[up3, hi] + om[1, :, mid].astype(F32)).astype(BF16)
        push("o1", (j, 1, 1), os.at[up3, hi], orx.at[1, :, hi], col(3))

    def backward(r):
        for h in (1, 0) if r == 1 else (0, 1):
            cols = pl.ds(h * 256, 256)
            acc = dot(cotg[...].reshape(512, 2048), wg[r, cols, :], 1, 1)
            if r == 0:
                gf[:, cols] = acc
            elif r == 2:
                gs[1, :, cols] = acc.astype(BF16)
                push("gm", (h,), gs.at[1, :, cols], gm.at[h], row(1 if h == 0 else 3))
            elif (r, h) in ((1, 0), (3, 1)):
                gt[h] = acc
            else:
                gs[r - 1, :, cols] = acc.astype(BF16)
                push("g", (1 - h, h), gs.at[r - 1, :, cols], gr.at[1 - h, :, cols], row(r))

    def backward_on(h):
        cols = pl.ds(h * 256, 256)
        arrive("gm", (h,))
        gs[2 * h, :, cols] = (gt[h] + gm[h].astype(F32)).astype(BF16)
        push("g", (h, h), gs.at[2 * h, :, cols], gr.at[h, :, cols], row(1 if h == 0 else 3))

    eight = slab(c, 8)

    def block(yy):
        return gb.at[eight, pl.ds(pl.multiple_of(x * 2048 + yy * 512, 512), 512)]

    def output(j):
        cols = pl.ds(j * CW, CW)
        for k in (0, 1):
            for h in (0, 1):
                arrive("o1", (j, k, h))
        acc = of[slab(y, 128), cols] + orx[0, :, cols].astype(F32) + orx[1, :, cols].astype(F32)
        acc += SCALE * dot(lowv[:, slab(y, 128)], upv[:, cols], 0, 0)
        ob[:, cols] = acc.astype(BF16)
        here = pl.ds(pl.multiple_of(x * 2048 + j * CW, CW), CW)
        for d in (2, 1, 3):
            push("o2", (j, d), ob.at[slab(lax.rem(x + d, 4), 32), cols], out.at[:, here], row(d))
        return local(ob.at[slab(x, 32), cols], out.at[:, here])

    ld_w.wait()
    spread_end("c2")
    weight(0, 1)
    backward(2)
    step_z(3, 4)
    step_z(3, 5)

    for d in (1, 2, 3):
        arrive("ly", (d,))
        arrive("lgy", (d,))
    lowv[...] = ((ly[0] + ly[1]) + (ly[2] + ly[3])).astype(BF16)
    parts_a = [dot(lgv[r], tokg[slab(lax.rem(y + r, 4), 128), pl.ds(0, 512)], 1, 0) for r in range(4)]
    gab[0] = (parts_a[0] + parts_a[1]) + (parts_a[2] + parts_a[3])
    parts_b = [dot(lowv[:, slab(lax.rem(y + r, 4), 128)], cotg[r, :, slab(y, 512)], 1, 0) for r in range(4)]
    gab[1] = (parts_b[0] + parts_b[1]) + (parts_b[2] + parts_b[3])
    push("sb", (0,), gab.at[1 - c], sibin, sib)
    step_z(4, 2)
    step_z(4, 3)
    spread_end("t")
    weight(2, 3)
    forward(0)
    step_z(4, 4)
    step_z(4, 5)
    arrive("sb", (0,))
    zin[z] = gab[c] + sibin[...]
    for d in range(1, 8):
        push("z", (d,), zin.at[z], zin.at[z], zed(d))
    forward(1)
    forward_on(0)
    weight(4, 5)
    backward(1)
    backward(3)
    forward_on(1)
    forward(2)
    backward_on(0)
    backward_on(1)
    for d in range(1, 8):
        arrive("z", (d,), zin.at[lax.rem(z + 8 - d, 8)])
    total = zin[0]
    for i in range(1, 8):
        total = total + zin[i]
    gav[c] = total * FACTOR
    push("sb", (1,), gav.at[c], gav.at[c], sib)
    own = [output(0)]
    arrive("sb", (1,), gav.at[1 - c])
    ga_out = local(gav.at[0], ga)
    for d in (1, 2, 3):
        push("gy", (d,), gav.at[1, eight, :], block(y), col(d))
    gb_own = local(gav.at[1, eight, :], block(y))
    forward(3)
    forward_on(2)
    own.append(output(1))
    forward_on(3)
    backward(0)
    gb_own.wait()
    for d in (1, 2, 3):
        arrive("gy", (d,), block(lax.rem(y + 4 - d, 4)))
    for d in (1, 2, 3):
        push("gx", (d,), gb.at[eight, slab(x, 2048)], gb.at[eight, slab(x, 2048)], row(d))
    own.append(output(2))
    own.append(output(3))
    for d in (1, 2, 3):
        arrive("gx", (d,), gb.at[eight, slab(lax.rem(x + 4 - d, 4), 2048)])
    push("sb", (2,), gb.at[eight, :], gb.at[eight, :], sib)

    for h in range(2):
        cols = pl.ds(h * 256, 256)
        arrive("g", (0, h))
        arrive("g", (1, h))
        for q in range(4):
            rows = pl.ds(q * 128, 128)
            acc = gf[rows, cols] + gr[0, rows, cols].astype(F32) + gr[1, rows, cols].astype(F32)
            acc += SCALE * dot(lgv[q], dnv[:, cols], 0, 0)
            tgv[slab(lax.rem(y + q, 4), 128), cols] = acc.astype(BF16)
    tg_out = local(tgv, tg)

    arrive("sb", (2,), gb.at[slab(1 - c, 8), :])
    for j in range(CHUNKS):
        own[j].wait()
        for d in (1, 2, 3):
            there = pl.ds(pl.multiple_of(lax.rem(x + 4 - d, 4) * 2048 + j * CW, CW), CW)
            arrive("o2", (j, d), out.at[:, there])
    tg_out.wait()
    ga_out.wait()
    for cp in sends:
        cp.wait_send()


def finish(a, b, c, d, oa, ob, oc, od, va, vb, vc, vd, sem):
    loads = [pltpu.make_async_copy(s, v, sem.at[0, i]) for i, (s, v) in enumerate(((a, va), (b, vb), (c, vc), (d, vd)))]
    stores = [pltpu.make_async_copy(v, o, sem.at[1, i]) for i, (v, o) in enumerate(((va, oa), (vb, ob), (vc, oc), (vd, od)))]
    for cp in loads:
        cp.start()
    for load, store in zip(loads, stores):
        load.wait()
        store.start()
    for cp in stores:
        cp.wait()


def per_device(tokens, weight, down_adapter, up_adapter, cotangent):
    dma = pltpu.SemaphoreType.DMA
    any_ = pl.BlockSpec(memory_space=pl.ANY)
    results = (
        jax.ShapeDtypeStruct((32, 8192), BF16),
        jax.ShapeDtypeStruct((512, 512), BF16),
        jax.ShapeDtypeStruct((16, 512), F32),
        jax.ShapeDtypeStruct((16, 8192), F32),
    )
    made = pl.pallas_call(
        kernel,
        out_shape=results,
        in_specs=[any_] * 5,
        out_specs=(any_,) * 4,
        scratch_shapes=[pltpu.VMEM(*b) for b in BUFFERS.values()]
        + [dma((16,))]
        + [dma(shape) for shape in TRANSFERS.values() for _ in range(2)],
        compiler_params=pltpu.CompilerParams(collective_id=0, has_side_effects=True, vmem_limit_bytes=56 * 2**20),
        name="projection",
    )(tokens, weight, down_adapter.T, up_adapter, cotangent)
    output, token_gradient, grad_a, grad_b = pl.pallas_call(
        finish,
        out_shape=results,
        in_specs=[any_] * 4,
        out_specs=(any_,) * 4,
        scratch_shapes=[pltpu.VMEM(r.shape, r.dtype) for r in results] + [dma((2, 4))],
        name="results",
    )(*made)
    return output, token_gradient, grad_a.T, grad_b


def solution(mesh):
    placed = (
        P("dp", "tensor"),
        P("tensor", None),
        P("tensor", None),
        P(),
        P(("dp", "tensor"), None),
    )
    return jax.shard_map(
        per_device,
        mesh=mesh,
        in_specs=placed,
        out_specs=(P(("dp", "tensor"), None), P("dp", "tensor"), P("tensor", None), P()),
        check_vma=False,
    )
```
